512 devices in a mesh: ctx: 64 (over z_hi, x, y), tp: 8 (over z_lo, core).
Axes of the slice: x: 4, y: 4, z: 16 (z_hi: 4, z_lo: 4; z = z_hi * 4 + z_lo), core: 2. Of those that a mesh axis runs over, the one named last changes fastest.
Arguments:
- tokens: bfloat16 [16384, 2688], P(('ctx', 'tp')), may hold values from -6 to 6
- result_grad: bfloat16 [16384, 2688], P(('ctx', 'tp')), may hold values from -6 to 6
- query_weight: bfloat16 [2688, 2048], P(None, 'tp'), may hold values from -0.125 to 0.125
- key_weight: bfloat16 [2688, 1024], P(None, 'tp'), may hold values from -0.125 to 0.125
- value_weight: bfloat16 [2688, 1024], P(None, 'tp'), may hold values from -0.125 to 0.125
- output_weight: bfloat16 [2048, 2688], P('tp'), may hold values from -0.5 to 0.5
- query_gain: float32 [128], replicated, may hold values from 0.5 to 1.5
- key_gain: float32 [128], replicated, may hold values from 0.5 to 1.5
Outputs:
- layer_output: bfloat16 [16384, 2688], P(('ctx', 'tp'))
- tokens_grad: bfloat16 [16384, 2688], P(('ctx', 'tp'))
The draws below stay inside these ranges and needn't reach their ends.
All inputs are finite; a program needn't handle non-finite values.
Results may differ from the reference program's by a relative error of at most 0.012.
Values may be sent and summed in bfloat16 or wider, within the bound.
No kernel may reach another device: no remote copies, remote signals or barrier semaphores. Data moves between devices by JAX's collectives and lax.ppermute only.
A program may use at most 64 MiB of HBM per device.

```python
import jax
import jax.numpy as jnp
from jax import lax

D = 2688
HEAD = 128
WINDOW = 1024
T_DEV = 256
TOKENS = 16384
QHEADS = 16
KVHEADS = 8
N_TP = 8


def shard_levels(stream_key, extent, split, low, top_value):
    gain = 1.0
    for position, blocks in split:
        draws = jax.random.uniform(jax.random.fold_in(jax.random.fold_in(stream_key, 6), position), (blocks,), jnp.float32, low / len(split), top_value / len(split))
        gain = gain * jnp.repeat(jnp.exp(draws), extent[position] // blocks).reshape((-1,) + (1,) * (len(extent) - 1 - position))
    return gain


def noise(stream_key, shape, width, reach, cuts=(), held_as=jnp.bfloat16):
    gain = shard_levels(stream_key, shape, cuts, -0.22, 0.18) if cuts else 1.0
    array = jax.random.normal(stream_key, shape, jnp.float32) * width * gain
    return jnp.minimum(jnp.maximum(array, -reach), reach).astype(held_as)


def setup_inputs(seed: int = 0) -> dict:
    keys = jax.random.split(jax.random.key(seed), 9)
    return {
        "tokens": noise(keys[0], (TOKENS, D), 1.0, 6.0, ((0, 512),)),
        "result_grad": noise(keys[1], (TOKENS, D), 1.0, 6.0, ((0, 512),)),
        "query_weight": noise(keys[2], (D, QHEADS * HEAD), D ** -0.5, 0.125, ((1, 8),)),
        "key_weight": noise(keys[3], (D, KVHEADS * HEAD), D ** -0.5, 0.125, ((1, 8),)),
        "value_weight": noise(keys[4], (D, KVHEADS * HEAD), D ** -0.5, 0.125, ((1, 8),)),
        "output_weight": noise(keys[5], (QHEADS * HEAD, D), HEAD ** -0.5, 0.5, ((0, 8),)),
        "query_gain": jnp.clip(1.0 + 0.1 * jax.random.normal(keys[6], (HEAD,), jnp.float32), 0.5, 1.5),
        "key_gain": jnp.clip(1.0 + 0.1 * jax.random.normal(keys[7], (HEAD,), jnp.float32), 0.5, 1.5),
    }


norm_epsilon = 1e-06
score_scale = 168.0 ** (-0.5)
rope_theta = 10000.0

def rope_tables(positions, head_size):
    half_size = head_size // 2
    exponent = jnp.arange(half_size, dtype=jnp.float32) * (2.0 / head_size)
    frequency = jnp.power(jnp.float32(rope_theta), -exponent)
    angles = positions.astype(jnp.float32)[:, None] * frequency[None, :]
    return (jnp.cos(angles), jnp.sin(angles))

def norm_rope(raw_proj, scale_gain, cosines, sines):
    row_count = raw_proj.shape[0]
    head_size = scale_gain.shape[0]
    split_heads = raw_proj.reshape(row_count, -1, head_size)
    mean_square = lax.optimization_barrier(jnp.mean(split_heads * split_heads, axis=-1, keepdims=True))
    normed = split_heads * lax.rsqrt(mean_square + norm_epsilon) * scale_gain.astype(jnp.float32)
    half_size = head_size // 2
    low_half = normed[..., :half_size]
    high_half = normed[..., half_size:]
    cosine_b = cosines[:, None, :]
    sine_b = sines[:, None, :]
    return jnp.concatenate([low_half * cosine_b - high_half * sine_b, high_half * cosine_b + low_half * sine_b], axis=-1)

def attend(queries, keys_all, values_all, out_grad, query_first, key_first):
    query_count = queries.shape[0]
    key_count = keys_all.shape[0]
    queries_f = queries.astype(jnp.float32)
    keys_f = keys_all.astype(jnp.float32)
    values_f = values_all.astype(jnp.float32)
    out_grad_f = out_grad.astype(jnp.float32)
    scores = jnp.einsum('qkgh,ckh->kgqc', queries_f, keys_f) * score_scale
    query_pos = query_first + jnp.arange(query_count, dtype=jnp.int32)
    key_pos = key_first + jnp.arange(key_count, dtype=jnp.int32)
    distance = query_pos[:, None] - key_pos[None, :]
    allowed = (distance >= 0) & (distance < WINDOW) & (key_pos[None, :] >= 0)
    weights_raw = jnp.where(allowed, jnp.exp(scores), jnp.float32(0.0))
    denominator = lax.optimization_barrier(jnp.sum(weights_raw, axis=-1, keepdims=True))
    weights_soft = weights_raw / denominator
    weights_low = lax.optimization_barrier(weights_soft.astype(jnp.bfloat16))
    weights_low_f = weights_low.astype(jnp.float32)
    attended = lax.optimization_barrier(jnp.einsum('kgqc,ckh->qkgh', weights_low_f, values_f).astype(jnp.bfloat16))
    row_dots = lax.optimization_barrier(jnp.sum(out_grad_f * attended.astype(jnp.float32), axis=-1))
    prob_grad = jnp.einsum('qkgh,ckh->kgqc', out_grad_f, values_f)
    centered = prob_grad - jnp.transpose(row_dots, (1, 2, 0))[..., None]
    score_grad = lax.optimization_barrier((weights_soft * centered * score_scale).astype(jnp.bfloat16))
    score_grad_f = score_grad.astype(jnp.float32)
    query_grad = jnp.einsum('kgqc,ckh->qkgh', score_grad_f, keys_f)
    key_grad = jnp.einsum('kgqc,qkgh->ckh', score_grad_f, queries_f)
    value_grad = jnp.einsum('kgqc,qkgh->ckh', weights_low_f, out_grad_f)
    return (attended, query_grad, key_grad, value_grad)

def group_pass(tokens, result_grad, query_weight, key_weight, value_weight, output_weight, query_gain, key_gain):
    token_count = tokens.shape[0]
    kv_count = key_weight.shape[1] // HEAD
    per_kv = query_weight.shape[1] // key_weight.shape[1]
    positions = jnp.arange(token_count, dtype=jnp.int32)
    cosines, sines = rope_tables(positions, HEAD)
    query_raw = jnp.dot(tokens, query_weight, preferred_element_type=jnp.float32)
    key_raw = jnp.dot(tokens, key_weight, preferred_element_type=jnp.float32)
    value_raw = jnp.dot(tokens, value_weight, preferred_element_type=jnp.float32)
    queries = norm_rope(query_raw, query_gain, cosines, sines).astype(jnp.bfloat16).reshape(token_count, kv_count, per_kv, HEAD)
    keys_all = norm_rope(key_raw, key_gain, cosines, sines).astype(jnp.bfloat16)
    values_all = value_raw.astype(jnp.bfloat16).reshape(token_count, kv_count, HEAD)
    out_grad = jnp.dot(result_grad, output_weight.T, preferred_element_type=jnp.float32).astype(jnp.bfloat16)
    out_grad = out_grad.reshape(token_count, kv_count, per_kv, HEAD)
    padding = jnp.zeros((WINDOW, kv_count, HEAD), jnp.bfloat16)
    keys_pad = jnp.concatenate([padding, keys_all], axis=0)
    values_pad = jnp.concatenate([padding, values_all], axis=0)

    def one_block(running, block_index):
        key_acc, value_acc = running
        first_row = (block_index * T_DEV).astype(jnp.int32)
        query_block = lax.dynamic_slice_in_dim(queries, first_row, T_DEV, 0)
        grad_block = lax.dynamic_slice_in_dim(out_grad, first_row, T_DEV, 0)
        key_block = lax.dynamic_slice_in_dim(keys_pad, first_row, WINDOW + T_DEV, 0)
        value_block = lax.dynamic_slice_in_dim(values_pad, first_row, WINDOW + T_DEV, 0)
        attended, query_grad, key_grad, value_grad = attend(query_block, key_block, value_block, grad_block, first_row, first_row - WINDOW)
        key_acc = lax.dynamic_update_slice_in_dim(key_acc, lax.dynamic_slice_in_dim(key_acc, first_row, WINDOW + T_DEV, 0) + key_grad, first_row, 0)
        value_acc = lax.dynamic_update_slice_in_dim(value_acc, lax.dynamic_slice_in_dim(value_acc, first_row, WINDOW + T_DEV, 0) + value_grad, first_row, 0)
        return ((key_acc, value_acc), (attended, query_grad))
    zeros_acc = jnp.zeros((WINDOW + token_count, kv_count, HEAD), jnp.float32)
    block_ids = jnp.arange(token_count // T_DEV, dtype=jnp.int32)
    (key_acc, value_acc), (attended, query_grad) = lax.scan(one_block, (zeros_acc, zeros_acc), block_ids)
    attended_flat = attended.reshape(token_count, -1)
    query_grad = query_grad.reshape(token_count, -1, HEAD)

    def query_shape(raw_proj):
        return norm_rope(raw_proj, query_gain, cosines, sines)

    def key_shape(raw_proj):
        return norm_rope(raw_proj, key_gain, cosines, sines)
    query_back = jax.vjp(query_shape, query_raw)[1](query_grad)[0].astype(jnp.bfloat16)
    key_back = jax.vjp(key_shape, key_raw)[1](key_acc[WINDOW:])[0].astype(jnp.bfloat16)
    value_back = value_acc[WINDOW:].reshape(token_count, -1).astype(jnp.bfloat16)
    out_part = jnp.dot(attended_flat, output_weight, preferred_element_type=jnp.float32).astype(jnp.bfloat16)
    grad_part = jnp.dot(query_back, query_weight.T, preferred_element_type=jnp.float32)
    grad_part = grad_part + jnp.dot(key_back, key_weight.T, preferred_element_type=jnp.float32)
    grad_part = grad_part + jnp.dot(value_back, value_weight.T, preferred_element_type=jnp.float32)
    return (out_part, grad_part.astype(jnp.bfloat16))

def reference(tokens, result_grad, query_weight, key_weight, value_weight, output_weight, query_gain, key_gain):
    query_cols = query_weight.shape[1] // N_TP
    kv_cols = key_weight.shape[1] // N_TP
    out_sum = tokens.astype(jnp.float32)
    grad_sum = result_grad.astype(jnp.float32)
    for group_index in range(N_TP):
        query_part = query_weight[:, group_index * query_cols:(group_index + 1) * query_cols]
        key_part = key_weight[:, group_index * kv_cols:(group_index + 1) * kv_cols]
        value_part = value_weight[:, group_index * kv_cols:(group_index + 1) * kv_cols]
        output_part = output_weight[group_index * query_cols:(group_index + 1) * query_cols]
        out_part, grad_part = group_pass(tokens, result_grad, query_part, key_part, value_part, output_part, query_gain, key_gain)
        out_sum = out_sum + out_part.astype(jnp.float32)
        grad_sum = grad_sum + grad_part.astype(jnp.float32)
    return (out_sum.astype(jnp.bfloat16), grad_sum.astype(jnp.bfloat16))
```

```python
import jax
import jax.numpy as jnp
from jax import lax
from jax.sharding import Mesh, PartitionSpec as P

WINDOW = 1024
ALL = ("zh", "x", "y", "zl", "c")
TP = ("zl", "c")

norm_epsilon = 1e-06
score_scale = 168.0 ** (-0.5)
rope_theta = 10000.0
f32 = jnp.float32
bf16 = jnp.bfloat16


def swap_cores(block):
    return lax.ppermute(block, "c", [(0, 1), (1, 0)])


def shift_rows(block, step):
    count = lax.axis_size(("zh", "x"))
    route = [(i, i + step) for i in range(count) if 0 <= i + step < count]
    return lax.ppermute(block, ("zh", "x"), route)


def rope_tables(positions, head_size):
    half_size = head_size // 2
    exponent = jnp.arange(half_size, dtype=f32) * (2.0 / head_size)
    frequency = jnp.power(f32(rope_theta), -exponent)
    angles = positions.astype(f32)[:, None] * frequency[None, :]
    return (jnp.cos(angles), jnp.sin(angles))


def norm_rope(raw_proj, scale_gain, cosines, sines):
    row_count = raw_proj.shape[0]
    head_size = scale_gain.shape[0]
    split_heads = raw_proj.reshape(row_count, -1, head_size)
    mean_square = jnp.mean(split_heads * split_heads, axis=-1, keepdims=True)
    normed = split_heads * lax.rsqrt(mean_square + norm_epsilon) * scale_gain
    half_size = head_size // 2
    low_half = normed[..., :half_size]
    high_half = normed[..., half_size:]
    cosine_b = cosines[:, None, :]
    sine_b = sines[:, None, :]
    return jnp.concatenate(
        [low_half * cosine_b - high_half * sine_b, high_half * cosine_b + low_half * sine_b],
        axis=-1,
    )


def attend(queries, keys_all, values_all, out_grad, query_pos, key_pos):
    scores = jnp.einsum("qgh,ch->gqc", queries, keys_all, preferred_element_type=f32) * score_scale
    distance = query_pos[:, None] - key_pos[None, :]
    allowed = (distance >= 0) & (distance < WINDOW) & (key_pos[None, :] >= 0)
    weights_raw = jnp.where(allowed, jnp.exp(scores), f32(0.0))
    denominator = jnp.sum(weights_raw, axis=-1, keepdims=True)
    weights_soft = weights_raw / denominator
    weights_low = weights_soft.astype(bf16)
    attended = lax.optimization_barrier(
        jnp.einsum("gqc,ch->qgh", weights_low, values_all, preferred_element_type=f32).astype(bf16)
    )
    row_dots = jnp.sum(out_grad.astype(f32) * attended.astype(f32), axis=-1)
    prob_grad = jnp.einsum("qgh,ch->gqc", out_grad, values_all, preferred_element_type=f32)
    centered = prob_grad - jnp.transpose(row_dots, (1, 0))[..., None]
    score_grad = (weights_soft * centered * score_scale).astype(bf16)
    query_grad = jnp.einsum("gqc,ch->qgh", score_grad, keys_all, preferred_element_type=f32)
    key_grad = jnp.einsum("gqc,qgh->ch", score_grad, queries, preferred_element_type=f32)
    value_grad = jnp.einsum("gqc,qgh->ch", weights_low, out_grad, preferred_element_type=f32)
    return (attended, query_grad, key_grad, value_grad)


def on_device(
    tokens, result_grad, query_weight, key_weight, value_weight, output_weight, query_gain, key_gain
):
    local_rows, width = tokens.shape
    n_zl = lax.axis_size("zl")
    n_y = lax.axis_size("y")
    row_count = local_rows * n_zl * lax.axis_size("c")
    head_size = query_gain.shape[0]
    core = lax.axis_index("c")
    y = lax.axis_index("y")
    query_cols = query_weight.shape[1]
    kv_cols = key_weight.shape[1]

    def order_rows(mine, other):
        cols = mine.shape[-1]
        first = jnp.where(core == 0, mine, other).reshape(n_zl, 1, local_rows, cols)
        second = jnp.where(core == 0, other, mine).reshape(n_zl, 1, local_rows, cols)
        return jnp.concatenate([first, second], axis=1).reshape(row_count, cols)

    gradients_part = lax.all_gather(result_grad, TP, axis=0, tiled=True)
    mine = lax.all_to_all(jnp.tile(tokens, (n_zl, 1)), "zl", 0, 0, tiled=True)
    other = swap_cores(mine)
    both = jnp.concatenate([mine, other], axis=0)

    def project(weight):
        rows = jnp.dot(both, weight, preferred_element_type=f32)
        half = rows.shape[0] // 2
        return order_rows(rows[:half], rows[half:])

    key_raw = project(key_weight)
    values_own = project(value_weight).astype(bf16)
    block = lax.axis_index(("zh", "x")) * n_y + y
    row_first = block * row_count
    positions = row_first + jnp.arange(row_count, dtype=jnp.int32)
    cosines, sines = rope_tables(positions, head_size)
    keys_own = norm_rope(key_raw, key_gain, cosines, sines).astype(bf16).reshape(row_count, head_size)
    own_kv = jnp.concatenate([keys_own, values_own], axis=1)
    above_kv = shift_rows(own_kv, 1)
    query_raw = project(query_weight)
    queries = (
        norm_rope(query_raw, query_gain, cosines, sines).astype(bf16).reshape(row_count, -1, head_size)
    )
    targets = jnp.arange(n_y, dtype=jnp.int32)
    outgoing = jnp.where((targets > y)[:, None, None], own_kv[None], above_kv[None])
    halo_kv = lax.all_to_all(outgoing, "y", 0, 0, tiled=True).reshape(n_y * row_count, 2 * head_size)
    base = lax.axis_index(("zh", "x")) * n_y * row_count
    halo_pos = (
        base
        + jnp.arange(n_y * row_count, dtype=jnp.int32)
        - jnp.where(jnp.repeat(targets, row_count) >= y, WINDOW, 0)
    )
    key_pos = jnp.concatenate([halo_pos, positions])
    all_kv = jnp.concatenate([halo_kv, own_kv], axis=0)

    out_grad = (
        jnp.einsum("nd,hd->nh", gradients_part, output_weight, preferred_element_type=f32)
        .astype(bf16)
        .reshape(row_count, -1, head_size)
    )
    attended, query_grad, key_grad, value_grad = attend(
        queries, all_kv[:, :head_size], all_kv[:, head_size:], out_grad, positions, key_pos
    )
    attended_flat = attended.reshape(row_count, query_cols)
    out_part = jnp.dot(attended_flat, output_weight, preferred_element_type=f32).astype(bf16)
    out_sum = lax.psum_scatter(out_part, TP, scatter_dimension=0, tiled=True).astype(f32)

    kv_grad = jnp.concatenate([key_grad, value_grad], axis=1)
    halo_grad = kv_grad[: n_y * row_count].astype(bf16).reshape(n_y, row_count, 2 * head_size)
    back = lax.all_to_all(halo_grad, "y", 0, 0, tiled=True).astype(f32)
    later = (targets > y)[:, None, None]
    back_own = jnp.sum(jnp.where(later, back, 0.0), axis=0)
    back_above = jnp.sum(jnp.where(later, 0.0, back), axis=0).astype(bf16)
    from_below = shift_rows(back_above, -1).astype(f32)

    def query_shape(raw_proj):
        return norm_rope(raw_proj, query_gain, cosines, sines)

    def key_shape(raw_proj):
        return norm_rope(raw_proj, key_gain, cosines, sines)

    query_back = jax.vjp(query_shape, query_raw)[1](query_grad)[0].astype(bf16)
    kv_own = kv_grad[n_y * row_count :] + back_own + from_below
    key_back = jax.vjp(key_shape, key_raw)[1](kv_own[:, None, :head_size])[0].astype(bf16)
    value_back = kv_own[:, head_size:].astype(bf16)

    def back_rows(which):
        def pick(array):
            split = array.reshape(n_zl, 2, local_rows, array.shape[-1])
            return lax.dynamic_index_in_dim(split, which, 1, keepdims=False).reshape(
                n_zl * local_rows, array.shape[-1]
            )

        dot = lambda a, w: jnp.einsum("nh,dh->nd", pick(a), w, preferred_element_type=f32)
        return (
            dot(query_back, query_weight) + dot(key_back, key_weight) + dot(value_back, value_weight)
        )

    given = swap_cores(back_rows(1 - core).astype(bf16))
    pair = (back_rows(core) + given.astype(f32)).astype(bf16)
    pieces = lax.all_to_all(pair, "zl", 0, 0, tiled=True).reshape(n_zl, local_rows, width)
    grad_sum = jnp.sum(pieces.astype(f32), axis=0)
    layer_output = (tokens.astype(f32) + out_sum).astype(bf16)
    tokens_grad = (result_grad.astype(f32) + grad_sum).astype(bf16)
    return (layer_output, tokens_grad)


def solution(mesh):
    fine = Mesh(mesh.devices.reshape(4, 4, 4, 4, 2), ALL)
    in_specs = (
        P(ALL, None),
        P(ALL, None),
        P(None, TP),
        P(None, TP),
        P(None, TP),
        P(TP, None),
        P(),
        P(),
    )
    out_specs = (P(ALL, None), P(ALL, None))
    return jax.shard_map(
        on_device, mesh=fine, in_specs=in_specs, out_specs=out_specs, check_vma=False
    )
```

```python
import functools

import jax
import jax.numpy as jnp
from jax import lax
from jax.experimental import pallas as pl
from jax.experimental.pallas import tpu as pltpu
from jax.sharding import Mesh, PartitionSpec as P

WINDOW = 1024
ALL = ("zh", "x", "y", "zl", "c")
TP = ("zl", "c")

norm_epsilon = 1e-06
score_scale = 168.0 ** (-0.5)
rope_theta = 10000.0
f32 = jnp.float32
bf16 = jnp.bfloat16
i32 = jnp.int32

ROWS = 256
HALF = 128
PIECE = 32
HEAD = 128
Q_HEADS = 2
CHUNKS = 4


def swap_cores(block):
    return lax.ppermute(block, "c", [(0, 1), (1, 0)])


def shift_rows(block, step):
    count = lax.axis_size(("zh", "x"))
    route = [(i, i + step) for i in range(count) if 0 <= i + step < count]
    return lax.ppermute(block, ("zh", "x"), route)


def natural(index):
    return ((index >> 5) & 3) * 64 + (index >> 7) * 32 + (index & 31)


def rope_tables(positions):
    half_size = HEAD // 2
    exponent = jnp.arange(half_size, dtype=f32) * (2.0 / HEAD)
    frequency = jnp.power(f32(rope_theta), -exponent)
    angles = positions.astype(f32)[:, None] * frequency[None, :]
    cosines, sines = jnp.cos(angles), jnp.sin(angles)
    return (
        jnp.concatenate([cosines, cosines], axis=1),
        jnp.concatenate([-sines, sines], axis=1),
    )


def dot_nn(a, b):
    return lax.dot_general(a, b, (((1,), (0,)), ((), ())), preferred_element_type=f32)


def dot_nt(a, b):
    return lax.dot_general(a, b, (((1,), (1,)), ((), ())), preferred_element_type=f32)


def dot_tn(a, b):
    return lax.dot_general(a, b, (((0,), (0,)), ((), ())), preferred_element_type=f32)


def norm_rope(raw, gain, cosines, sines):
    inverse = lax.rsqrt(jnp.mean(raw * raw, axis=-1, keepdims=True) + norm_epsilon)
    normed = raw * inverse * gain
    return normed * cosines + pltpu.roll(normed, HEAD // 2, 1) * sines


def norm_rope_back(raw, gain, cosines, sines, grad):
    inverse = lax.rsqrt(jnp.mean(raw * raw, axis=-1, keepdims=True) + norm_epsilon)
    normed_grad = (grad * cosines - pltpu.roll(grad, HEAD // 2, 1) * sines) * gain
    along = jnp.mean(raw * normed_grad, axis=-1, keepdims=True)
    return inverse * normed_grad - raw * (inverse * inverse * inverse * along)


def copies_kernel(tokens_ref, out_ref):
    for k in range(CHUNKS):
        out_ref[k] = tokens_ref[...]


def kv_kernel(place, mine, other, wk, wv, gain, cos, sin, kv_out, raw_out):
    for rows, which in ((mine, place[0]), (other, 1 - place[0])):
        at = pl.ds(pl.multiple_of(which * HALF, HALF), HALF)
        raw = dot_nn(rows[...], wk[...])
        raw_out[at, :] = raw
        kv_out[at, :HEAD] = norm_rope(raw, gain[...], cos[at, :], sin[at, :]).astype(bf16)
        kv_out[at, HEAD:] = dot_nn(rows[...], wv[...]).astype(bf16)


def q_kernel(place, mine, other, wq, gain, cos, sin, q_out, raw_out):
    for rows, which in ((mine, place[0]), (other, 1 - place[0])):
        at = pl.ds(pl.multiple_of(which * HALF, HALF), HALF)
        raw = dot_nn(rows[...], wq[...])
        raw_out[at, :] = raw
        for h in range(Q_HEADS):
            cols = slice(h * HEAD, (h + 1) * HEAD)
            q_out[at, cols] = norm_rope(raw[:, cols], gain[...], cos[at, :], sin[at, :]).astype(bf16)


def grad_kernel(rows, wo, out):
    got = dot_nt(rows[...], wo[...]).astype(bf16)
    for zl in range(4):
        for c in range(2):
            out[c * HALF + zl * PIECE : c * HALF + (zl + 1) * PIECE, :] = got[
                (zl * 2 + c) * PIECE : (zl * 2 + c + 1) * PIECE, :
            ]


def masks(place, key_axis):
    shape = (ROWS, ROWS)
    ahead = natural(lax.broadcasted_iota(i32, shape, key_axis)) - natural(
        lax.broadcasted_iota(i32, shape, 1 - key_axis)
    )
    everything, nothing = -4 * ROWS, 4 * ROWS
    allowed = []
    for k in range(CHUNKS):
        beyond = jnp.where(place[2] > 0, everything, nothing)
        limit = jnp.where(
            k < place[1], everything, jnp.where((k == place[1]) & (place[2] > 0), 0, beyond)
        )
        allowed.append(ahead > limit)
    allowed.append(ahead <= 0)
    return allowed


def kv_chunk(halo, own, k):
    return halo[k] if k < CHUNKS else own[...]


def forward_kernel(place, q, halo, own, attended_out, probs):
    allowed = masks(place, 1)
    for h in range(Q_HEADS):
        cols = slice(h * HEAD, (h + 1) * HEAD)
        query = q[:, cols]
        total = jnp.zeros((ROWS, 1), f32)
        for k in range(CHUNKS + 1):
            keys = kv_chunk(halo, own, k)[:, :HEAD]
            raw = jnp.where(allowed[k], jnp.exp(dot_nt(query, keys) * score_scale), 0.0)
            total = total + jnp.sum(raw, axis=1, keepdims=True)
            probs[k] = raw
        inverse = 1.0 / total
        result = jnp.zeros((ROWS, HEAD), f32)
        for k in range(CHUNKS + 1):
            low = (probs[k] * inverse).astype(bf16)
            result = result + dot_nn(low, kv_chunk(halo, own, k)[:, HEAD:])
        attended_out[:, cols] = result.astype(bf16)


def out_kernel(attended, wo, out):
    got = dot_nn(attended[...], wo[...]).astype(bf16)
    for zl in range(4):
        for c in range(2):
            out[(zl * 2 + c) * PIECE : (zl * 2 + c + 1) * PIECE, :] = got[
                c * HALF + zl * PIECE : c * HALF + (zl + 1) * PIECE, :
            ]


def backward_kernel(
    place, q, halo, own, grad, attended, q_raw, gain, cos, sin, q_back, halo_back, own_back, probs, dkv
):
    allowed = masks(place, 0)
    for h in range(Q_HEADS):
        cols = slice(h * HEAD, (h + 1) * HEAD)
        query, out_grad = q[:, cols], grad[:, cols]
        products = out_grad.astype(f32) * attended[:, cols].astype(f32)
        dots = jnp.sum(jnp.transpose(products), axis=0, keepdims=True)
        total = jnp.zeros((1, ROWS), f32)
        for k in range(CHUNKS + 1):
            keys = kv_chunk(halo, own, k)[:, :HEAD]
            raw = jnp.where(allowed[k], jnp.exp(dot_nt(keys, query) * score_scale), 0.0)
            total = total + jnp.sum(raw, axis=0, keepdims=True)
            probs[k] = raw
        inverse = 1.0 / total
        query_grad = jnp.zeros((ROWS, HEAD), f32)
        for k in range(CHUNKS + 1):
            kv = kv_chunk(halo, own, k)
            soft = probs[k] * inverse
            prob_grad = dot_nt(kv[:, HEAD:], out_grad)
            score_grad = (soft * (prob_grad - dots) * score_scale).astype(bf16)
            value_grad = dot_nn(soft.astype(bf16), out_grad)
            key_grad = dot_nn(score_grad, query)
            query_grad = query_grad + dot_tn(score_grad, kv[:, :HEAD])
            if h > 0:
                key_grad = key_grad + dkv[k, :, :HEAD]
                value_grad = value_grad + dkv[k, :, HEAD:]
            if h < Q_HEADS - 1:
                dkv[k, :, :HEAD] = key_grad
                dkv[k, :, HEAD:] = value_grad
            elif k < CHUNKS:
                halo_back[k, :, :HEAD] = key_grad.astype(bf16)
                halo_back[k, :, HEAD:] = value_grad.astype(bf16)
            else:
                own_back[:, :HEAD] = key_grad
                own_back[:, HEAD:] = value_grad
        q_back[:, cols] = norm_rope_back(
            q_raw[:, cols], gain[...], cos[...], sin[...], query_grad
        ).astype(bf16)


def gather_kernel(place, back, own_back, own_out, above_out):
    own = own_back[...]
    above = jnp.zeros((ROWS, 2 * HEAD), f32)
    for k in range(CHUNKS):
        later = k > place[1]
        piece = back[k].astype(f32)
        own = own + jnp.where(later, piece, 0.0)
        above = above + jnp.where(later, 0.0, piece)
    own_out[...] = own
    above_out[...] = above.astype(bf16)


def base_kernel(q_back, wq, out):
    out[...] = dot_nt(q_back[...], wq[...])


def end_rows(place, which, base, own, below, k_raw, gain, cos, sin, wk, wv):
    at = pl.ds(pl.multiple_of(which * HALF, HALF), HALF)
    total = own[at, :] + below[at, :].astype(f32)
    key_back = norm_rope_back(k_raw[at, :], gain[...], cos[at, :], sin[at, :], total[:, :HEAD])
    return (
        base[at, :]
        + dot_nt(key_back.astype(bf16), wk[...])
        + dot_nt(total[:, HEAD:].astype(bf16), wv[...])
    )


def end_given_kernel(place, base, own, below, k_raw, gain, cos, sin, wk, wv, given):
    given[...] = end_rows(
        place, 1 - place[0], base, own, below, k_raw, gain, cos, sin, wk, wv
    ).astype(bf16)


def end_pair_kernel(place, base, own, below, k_raw, gain, cos, sin, wk, wv, arrived, pair):
    rows = end_rows(place, place[0], base, own, below, k_raw, gain, cos, sin, wk, wv)
    pair[...] = (rows + arrived[...].astype(f32)).astype(bf16)


def sum_kernel(first, pieces, out):
    total = first[...].astype(f32)
    for k in range(CHUNKS):
        total = total + pieces[k].astype(f32)
    out[...] = total.astype(bf16)


def call(kernel, outs, *operands, scratch=(), flops=0):
    in_specs = [
        pl.BlockSpec(memory_space=pltpu.SMEM if a.dtype == i32 else pltpu.VMEM) for a in operands
    ]
    shapes = [jax.ShapeDtypeStruct(shape, dtype) for shape, dtype in outs]
    size = sum(a.size * a.dtype.itemsize for a in (*operands, *shapes))
    results = pl.pallas_call(
        kernel,
        out_shape=shapes,
        in_specs=in_specs,
        out_specs=[pl.BlockSpec(memory_space=pltpu.VMEM)] * len(shapes),
        scratch_shapes=scratch,
        compiler_params=pltpu.CompilerParams(vmem_limit_bytes=8 * 2**20),
        cost_estimate=pl.CostEstimate(flops=flops, bytes_accessed=size, transcendentals=0),
        name=kernel.__name__,
    )(*operands)
    return results[0] if len(results) == 1 else results


def on_device(
    tokens, result_grad, query_weight, key_weight, value_weight, output_weight, query_gain, key_gain
):
    width = tokens.shape[1]
    core, y = lax.axis_index("c"), lax.axis_index("y")
    block_row = lax.axis_index(("zh", "x"))
    place = jnp.stack([core, y, block_row]).astype(i32)
    query_gain, key_gain = query_gain[None], key_gain[None]
    positions = (block_row * CHUNKS + y) * ROWS + natural(jnp.arange(ROWS, dtype=i32))
    cos, sin = rope_tables(positions)

    gradients_part = lax.all_gather(result_grad, TP, axis=0, tiled=True)
    copies = call(copies_kernel, [((CHUNKS, PIECE, width), bf16)], tokens)
    mine = lax.all_to_all(copies, "zl", 0, 0, tiled=True).reshape(HALF, width)
    other = swap_cores(mine)
    own_kv, key_raw = call(
        kv_kernel,
        [((ROWS, 2 * HEAD), bf16), ((ROWS, HEAD), f32)],
        place, mine, other, key_weight, value_weight, key_gain, cos, sin,
    )
    above_kv = shift_rows(own_kv, 1)
    queries, query_raw = call(
        q_kernel,
        [((ROWS, Q_HEADS * HEAD), bf16), ((ROWS, Q_HEADS * HEAD), f32)],
        place, mine, other, query_weight, query_gain, cos, sin,
    )
    targets = jnp.arange(CHUNKS, dtype=i32)
    outgoing = jnp.where((targets > y)[:, None, None], own_kv[None], above_kv[None])
    halo = lax.all_to_all(outgoing, "y", 0, 0, tiled=True)
    out_grad = call(
        grad_kernel, [((ROWS, Q_HEADS * HEAD), bf16)], gradients_part, output_weight
    )
    probs = pltpu.VMEM((CHUNKS + 1, ROWS, ROWS), f32)
    attended = call(
        forward_kernel, [((ROWS, Q_HEADS * HEAD), bf16)], place, queries, halo, own_kv, scratch=[probs]
    )
    out_part = call(out_kernel, [((ROWS, width), bf16)], attended, output_weight)
    out_sum = lax.psum_scatter(out_part, TP, scatter_dimension=0, tiled=True)
    query_back, halo_back, own_back = call(
        backward_kernel,
        [
            ((ROWS, Q_HEADS * HEAD), bf16),
            ((CHUNKS, ROWS, 2 * HEAD), bf16),
            ((ROWS, 2 * HEAD), f32),
        ],
        place, queries, halo, own_kv, out_grad, attended, query_raw, query_gain, cos, sin,
        scratch=[probs, pltpu.VMEM((CHUNKS + 1, ROWS, 2 * HEAD), f32)],
    )
    back = lax.all_to_all(halo_back, "y", 0, 0, tiled=True)
    own_sum, above_sum = call(
        gather_kernel,
        [((ROWS, 2 * HEAD), f32), ((ROWS, 2 * HEAD), bf16)],
        place, back, own_back,
    )
    below = shift_rows(above_sum, -1)
    base = call(base_kernel, [((ROWS, width), f32)], query_back, query_weight)
    last = (place, base, own_sum, below, key_raw, key_gain, cos, sin, key_weight, value_weight)
    given = swap_cores(call(end_given_kernel, [((HALF, width), bf16)], *last))
    pair = call(end_pair_kernel, [((HALF, width), bf16)], *last, given)
    pieces = lax.all_to_all(pair.reshape(CHUNKS, PIECE, width), "zl", 0, 0, tiled=True)
    layer_output = (tokens.astype(f32) + out_sum.astype(f32)).astype(bf16)
    tokens_grad = call(sum_kernel, [((PIECE, width), bf16)], result_grad, pieces)
    return (layer_output, tokens_grad)


def solution(mesh):
    fine = Mesh(mesh.devices.reshape(4, 4, 4, 4, 2), ALL)
    in_specs = (
        P(ALL, None),
        P(ALL, None),
        P(None, TP),
        P(None, TP),
        P(None, TP),
        P(TP, None),
        P(),
        P(),
    )
    out_specs = (P(ALL, None), P(ALL, None))
    return jax.shard_map(
        on_device, mesh=fine, in_specs=in_specs, out_specs=out_specs, check_vma=False
    )
```

```python
import functools

import jax
import jax.numpy as jnp
from jax import lax
from jax.experimental import pallas as pl
from jax.experimental.pallas import tpu as pltpu
from jax.sharding import Mesh, PartitionSpec as P

WINDOW = 1024
ALL = ("zh", "x", "y", "zl", "c")
TP = ("zl", "c")

norm_epsilon = 1e-06
score_scale = 168.0 ** (-0.5)
rope_theta = 10000.0
f32 = jnp.float32
bf16 = jnp.bfloat16
i32 = jnp.int32

ROWS = 256
HALF = 128
PIECE = 32
HEAD = 128
Q_HEADS = 2
CHUNKS = 4
BLOCKED = True
VMEM_MIB = 20


def swap_cores(block):
    return lax.ppermute(block, "c", [(0, 1), (1, 0)])


def shift_rows(block, step):
    count = lax.axis_size(("zh", "x"))
    route = [(i, i + step) for i in range(count) if 0 <= i + step < count]
    return lax.ppermute(block, ("zh", "x"), route)


def natural(index):
    return ((index >> 5) & 3) * 64 + (index >> 7) * 32 + (index & 31)


def rope_tables(positions):
    half_size = HEAD // 2
    exponent = jnp.arange(half_size, dtype=f32) * (2.0 / HEAD)
    frequency = jnp.power(f32(rope_theta), -exponent)
    angles = positions.astype(f32)[:, None] * frequency[None, :]
    cosines, sines = jnp.cos(angles), jnp.sin(angles)
    return (
        jnp.concatenate([cosines, cosines], axis=1),
        jnp.concatenate([-sines, sines], axis=1),
    )


def dot_nn(a, b):
    return lax.dot_general(a, b, (((1,), (0,)), ((), ())), preferred_element_type=f32)


def dot_nt(a, b):
    return lax.dot_general(a, b, (((1,), (1,)), ((), ())), preferred_element_type=f32)


def dot_tn(a, b):
    return lax.dot_general(a, b, (((0,), (0,)), ((), ())), preferred_element_type=f32)


def norm_rope(raw, gain, cosines, sines):
    inverse = lax.rsqrt(jnp.mean(raw * raw, axis=-1, keepdims=True) + norm_epsilon)
    normed = raw * inverse * gain
    return normed * cosines + pltpu.roll(normed, HEAD // 2, 1) * sines


def norm_rope_back(raw, gain, cosines, sines, grad):
    inverse = lax.rsqrt(jnp.mean(raw * raw, axis=-1, keepdims=True) + norm_epsilon)
    normed_grad = (grad * cosines - pltpu.roll(grad, HEAD // 2, 1) * sines) * gain
    along = jnp.mean(raw * normed_grad, axis=-1, keepdims=True)
    return inverse * normed_grad - raw * (inverse * inverse * inverse * along)


def copies_kernel(tokens_ref, out_ref):
    for k in range(CHUNKS):
        out_ref[k] = tokens_ref[...]


def kv_kernel(place, mine, other, wk, wv, gain, cos, sin, kv_out, raw_out):
    for rows, which in ((mine, place[0]), (other, 1 - place[0])):
        at = pl.ds(pl.multiple_of(which * HALF, HALF), HALF)
        raw = dot_nn(rows[...], wk[...])
        raw_out[at, :] = raw
        kv_out[at, :HEAD] = norm_rope(raw, gain[...], cos[at, :], sin[at, :]).astype(bf16)
        kv_out[at, HEAD:] = dot_nn(rows[...], wv[...]).astype(bf16)


def q_kernel(place, mine, other, wq, gain, cos, sin, q_out, raw_out):
    for rows, which in ((mine, place[0]), (other, 1 - place[0])):
        at = pl.ds(pl.multiple_of(which * HALF, HALF), HALF)
        raw = dot_nn(rows[...], wq[...])
        raw_out[at, :] = raw
        for h in range(Q_HEADS):
            cols = slice(h * HEAD, (h + 1) * HEAD)
            q_out[at, cols] = norm_rope(raw[:, cols], gain[...], cos[at, :], sin[at, :]).astype(bf16)


def grad_kernel(rows, wo, out):
    got = dot_nt(rows[...], wo[...]).astype(bf16)
    for zl in range(4):
        for c in range(2):
            out[c * HALF + zl * PIECE : c * HALF + (zl + 1) * PIECE, :] = got[
                (zl * 2 + c) * PIECE : (zl * 2 + c + 1) * PIECE, :
            ]


def masks(place, key_axis):
    shape = (ROWS, ROWS)
    ahead = natural(lax.broadcasted_iota(i32, shape, key_axis)) - natural(
        lax.broadcasted_iota(i32, shape, 1 - key_axis)
    )
    everything, nothing = -4 * ROWS, 4 * ROWS
    allowed = []
    for k in range(CHUNKS):
        beyond = jnp.where(place[2] > 0, everything, nothing)
        limit = jnp.where(
            k < place[1], everything, jnp.where((k == place[1]) & (place[2] > 0), 0, beyond)
        )
        allowed.append(ahead > limit)
    allowed.append(ahead <= 0)
    return allowed


def kv_chunk(halo, own, k):
    return halo[k] if k < CHUNKS else own[...]


def out_kernel(attended, wo, out):
    got = dot_nn(attended[...], wo[...]).astype(bf16)
    for zl in range(4):
        for c in range(2):
            out[(zl * 2 + c) * PIECE : (zl * 2 + c + 1) * PIECE, :] = got[
                c * HALF + zl * PIECE : c * HALF + (zl + 1) * PIECE, :
            ]


def attention_kernel(
    place, q, halo, own, grad, q_raw, gain, cos, sin,
    attended_out, q_back, halo_back, own_back, probs, dkv,
):
    allowed = masks(place, 0)
    for h in range(Q_HEADS):
        cols = slice(h * HEAD, (h + 1) * HEAD)
        query, out_grad = q[:, cols], grad[:, cols]
        total = jnp.zeros((1, ROWS), f32)
        for k in range(CHUNKS + 1):
            keys = kv_chunk(halo, own, k)[:, :HEAD]
            raw = jnp.where(allowed[k], jnp.exp(dot_nt(keys, query) * score_scale), 0.0)
            total = total + jnp.sum(raw, axis=0, keepdims=True)
            probs[k] = raw
        inverse = 1.0 / total
        attended = jnp.zeros((HEAD, ROWS), f32)
        for k in range(CHUNKS + 1):
            soft = probs[k] * inverse
            probs[k] = soft
            low = soft.astype(bf16)
            attended = attended + dot_tn(kv_chunk(halo, own, k)[:, HEAD:], low)
            value_grad = dot_nn(low, out_grad)
            if h > 0:
                value_grad = value_grad + dkv[k, :, HEAD:]
            if h < Q_HEADS - 1:
                dkv[k, :, HEAD:] = value_grad
            elif k < CHUNKS:
                halo_back[k, :, HEAD:] = value_grad.astype(bf16)
            else:
                own_back[:, HEAD:] = value_grad
        attended_out[:, cols] = jnp.transpose(attended).astype(bf16)
        products = jnp.transpose(out_grad.astype(f32)) * attended.astype(bf16).astype(f32)
        dots = jnp.sum(products, axis=0, keepdims=True)
        query_grad = jnp.zeros((HEAD, ROWS), f32)
        for k in range(CHUNKS + 1):
            kv = kv_chunk(halo, own, k)
            prob_grad = dot_nt(kv[:, HEAD:], out_grad)
            score_grad = (probs[k] * (prob_grad - dots) * score_scale).astype(bf16)
            key_grad = dot_nn(score_grad, query)
            query_grad = query_grad + dot_tn(kv[:, :HEAD], score_grad)
            if h > 0:
                key_grad = key_grad + dkv[k, :, :HEAD]
            if h < Q_HEADS - 1:
                dkv[k, :, :HEAD] = key_grad
            elif k < CHUNKS:
                halo_back[k, :, :HEAD] = key_grad.astype(bf16)
            else:
                own_back[:, :HEAD] = key_grad
        q_back[:, cols] = norm_rope_back(
            q_raw[:, cols], gain[...], cos[...], sin[...], jnp.transpose(query_grad)
        ).astype(bf16)


def gather_kernel(place, back, own_back, own_out, above_out):
    own = own_back[...]
    above = jnp.zeros((ROWS, 2 * HEAD), f32)
    for k in range(CHUNKS):
        later = k > place[1]
        piece = back[k].astype(f32)
        own = own + jnp.where(later, piece, 0.0)
        above = above + jnp.where(later, 0.0, piece)
    own_out[...] = own
    above_out[...] = above.astype(bf16)


def base_kernel(q_back, wq, out):
    out[...] = dot_nt(q_back[...], wq[...])


def end_rows(place, which, base, own, below, k_raw, gain, cos, sin, wk, wv):
    at = pl.ds(pl.multiple_of(which * HALF, HALF), HALF)
    total = own[at, :] + below[at, :].astype(f32)
    key_back = norm_rope_back(k_raw[at, :], gain[...], cos[at, :], sin[at, :], total[:, :HEAD])
    return (
        base[at, :]
        + dot_nt(key_back.astype(bf16), wk[...])
        + dot_nt(total[:, HEAD:].astype(bf16), wv[...])
    )


def end_given_kernel(place, base, own, below, k_raw, gain, cos, sin, wk, wv, given):
    given[...] = end_rows(
        place, 1 - place[0], base, own, below, k_raw, gain, cos, sin, wk, wv
    ).astype(bf16)


def end_pair_kernel(place, base, own, below, k_raw, gain, cos, sin, wk, wv, arrived, pair):
    rows = end_rows(place, place[0], base, own, below, k_raw, gain, cos, sin, wk, wv)
    pair[...] = (rows + arrived[...].astype(f32)).astype(bf16)


def sum_kernel(first, pieces, out):
    total = first[...].astype(f32)
    for k in range(CHUNKS):
        total = total + pieces[k].astype(f32)
    out[...] = total.astype(bf16)


def call(kernel, outs, *operands, scratch=(), flops=0):
    in_specs = [
        pl.BlockSpec(memory_space=pltpu.SMEM if a.dtype == i32 else pltpu.VMEM) for a in operands
    ]
    shapes = [jax.ShapeDtypeStruct(shape, dtype) for shape, dtype in outs]
    out_specs = [pl.BlockSpec(memory_space=pltpu.VMEM)] * len(shapes)
    grid = ()
    if BLOCKED:
        whole = lambda a: pl.BlockSpec(a.shape, lambda i: (0,) * len(a.shape))
        in_specs = [
            pl.BlockSpec(memory_space=pltpu.SMEM) if a.dtype == i32 else whole(a) for a in operands
        ]
        out_specs = [whole(a) for a in shapes]
        grid = (1,)
    size = sum(a.size * a.dtype.itemsize for a in (*operands, *shapes))
    results = pl.pallas_call(
        kernel,
        out_shape=shapes,
        in_specs=in_specs,
        out_specs=out_specs,
        grid=grid,
        scratch_shapes=scratch,
        compiler_params=pltpu.CompilerParams(vmem_limit_bytes=VMEM_MIB * 2**20),
        cost_estimate=pl.CostEstimate(flops=flops, bytes_accessed=size, transcendentals=0),
        name=kernel.__name__,
    )(*operands)
    return results[0] if len(results) == 1 else results


def on_device(
    tokens, result_grad, query_weight, key_weight, value_weight, output_weight, query_gain, key_gain
):
    width = tokens.shape[1]
    core, y = lax.axis_index("c"), lax.axis_index("y")
    block_row = lax.axis_index(("zh", "x"))
    place = jnp.stack([core, y, block_row]).astype(i32)
    query_gain, key_gain = query_gain[None], key_gain[None]
    positions = (block_row * CHUNKS + y) * ROWS + natural(jnp.arange(ROWS, dtype=i32))
    cos, sin = rope_tables(positions)

    gradients_part = lax.all_gather(result_grad, TP, axis=0, tiled=True)
    copies = call(copies_kernel, [((CHUNKS, PIECE, width), bf16)], tokens)
    mine = lax.all_to_all(copies, "zl", 0, 0, tiled=True).reshape(HALF, width)
    other = swap_cores(mine)
    own_kv, key_raw = call(
        kv_kernel,
        [((ROWS, 2 * HEAD), bf16), ((ROWS, HEAD), f32)],
        place, mine, other, key_weight, value_weight, key_gain, cos, sin,
    )
    above_kv = shift_rows(own_kv, 1)
    queries, query_raw = call(
        q_kernel,
        [((ROWS, Q_HEADS * HEAD), bf16), ((ROWS, Q_HEADS * HEAD), f32)],
        place, mine, other, query_weight, query_gain, cos, sin,
    )
    targets = jnp.arange(CHUNKS, dtype=i32)
    outgoing = jnp.where((targets > y)[:, None, None], own_kv[None], above_kv[None])
    outgoing, queries = lax.optimization_barrier((outgoing, queries))
    halo = lax.all_to_all(outgoing, "y", 0, 0, tiled=True)
    halo, gradients_weight = lax.optimization_barrier((halo, output_weight))
    out_grad = call(
        grad_kernel, [((ROWS, Q_HEADS * HEAD), bf16)], gradients_part, gradients_weight
    )
    probs = pltpu.VMEM((CHUNKS + 1, ROWS, ROWS), f32)
    attended, query_back, halo_back, own_back = call(
        attention_kernel,
        [
            ((ROWS, Q_HEADS * HEAD), bf16),
            ((ROWS, Q_HEADS * HEAD), bf16),
            ((CHUNKS, ROWS, 2 * HEAD), bf16),
            ((ROWS, 2 * HEAD), f32),
        ],
        place, queries, halo, own_kv, out_grad, query_raw, query_gain, cos, sin,
        scratch=[probs, pltpu.VMEM((CHUNKS + 1, ROWS, 2 * HEAD), f32)],
    )
    out_part = call(out_kernel, [((ROWS, width), bf16)], attended, output_weight)
    out_sum = lax.psum_scatter(out_part, TP, scatter_dimension=0, tiled=True)
    back = lax.all_to_all(halo_back, "y", 0, 0, tiled=True)
    own_sum, above_sum = call(
        gather_kernel,
        [((ROWS, 2 * HEAD), f32), ((ROWS, 2 * HEAD), bf16)],
        place, back, own_back,
    )
    below = shift_rows(above_sum, -1)
    base = call(base_kernel, [((ROWS, width), f32)], query_back, query_weight)
    last = (place, base, own_sum, below, key_raw, key_gain, cos, sin, key_weight, value_weight)
    given = swap_cores(call(end_given_kernel, [((HALF, width), bf16)], *last))
    pair = call(end_pair_kernel, [((HALF, width), bf16)], *last, given)
    pieces = lax.all_to_all(pair.reshape(CHUNKS, PIECE, width), "zl", 0, 0, tiled=True)
    layer_output = (tokens.astype(f32) + out_sum.astype(f32)).astype(bf16)
    tokens_grad = call(sum_kernel, [((PIECE, width), bf16)], result_grad, pieces)
    return (layer_output, tokens_grad)


def solution(mesh):
    fine = Mesh(mesh.devices.reshape(4, 4, 4, 4, 2), ALL)
    in_specs = (
        P(ALL, None),
        P(ALL, None),
        P(None, TP),
        P(None, TP),
        P(None, TP),
        P(TP, None),
        P(),
        P(),
    )
    out_specs = (P(ALL, None), P(ALL, None))
    return jax.shard_map(
        on_device, mesh=fine, in_specs=in_specs, out_specs=out_specs, check_vma=False
    )
```

```python
import math

import jax
import jax.numpy as jnp
from jax import lax
from jax.experimental import pallas as pl
from jax.experimental.pallas import tpu as pltpu
from jax.sharding import Mesh, PartitionSpec as P

WINDOW = 1024
ALL = ("zh", "x", "y", "zl", "c")
TP = ("zl", "c")

norm_epsilon = 1e-06
score_scale = 168.0 ** (-0.5)
rope_theta = 10000.0
f32 = jnp.float32
bf16 = jnp.bfloat16
i32 = jnp.int32

ROWS = 256
HALF = 128
PIECE = 32
HEAD = 128
Q_HEADS = 2
CHUNKS = 4
BLOCKED = True
VMEM_MIB = 20


def swap_cores(block):
    return lax.ppermute(block, "c", [(0, 1), (1, 0)])


def shift_rows(block, step):
    count = lax.axis_size(("zh", "x"))
    route = [(i, i + step) for i in range(count) if 0 <= i + step < count]
    return lax.ppermute(block, ("zh", "x"), route)


def natural(index):
    return ((index >> 5) & 3) * 64 + (index >> 7) * 32 + (index & 31)


def rope_tables(positions):
    half_size = HEAD // 2
    exponent = jnp.arange(half_size, dtype=f32) * (2.0 / HEAD)
    frequency = jnp.power(f32(rope_theta), -exponent)
    angles = positions.astype(f32)[:, None] * frequency[None, :]
    cosines, sines = jnp.cos(angles), jnp.sin(angles)
    return (
        jnp.concatenate([cosines, cosines], axis=1),
        jnp.concatenate([-sines, sines], axis=1),
    )


def dot_nn(a, b):
    return lax.dot_general(a, b, (((1,), (0,)), ((), ())), preferred_element_type=f32)


def dot_nt(a, b):
    return lax.dot_general(a, b, (((1,), (1,)), ((), ())), preferred_element_type=f32)


def dot_tn(a, b):
    return lax.dot_general(a, b, (((0,), (0,)), ((), ())), preferred_element_type=f32)


def norm_rope(raw, gain, cosines, sines):
    inverse = lax.rsqrt(jnp.mean(raw * raw, axis=-1, keepdims=True) + norm_epsilon)
    normed = raw * inverse * gain
    return normed * cosines + pltpu.roll(normed, HEAD // 2, 1) * sines


def norm_rope_back(raw, gain, cosines, sines, grad):
    inverse = lax.rsqrt(jnp.mean(raw * raw, axis=-1, keepdims=True) + norm_epsilon)
    normed_grad = (grad * cosines - pltpu.roll(grad, HEAD // 2, 1) * sines) * gain
    along = jnp.mean(raw * normed_grad, axis=-1, keepdims=True)
    return inverse * normed_grad - raw * (inverse * inverse * inverse * along)


def copies_kernel(tokens_ref, out_ref):
    for k in range(CHUNKS):
        out_ref[k] = tokens_ref[...]


def kv_kernel(place, mine, other, wk, wv, gain, cos, sin, kv_out, raw_out):
    for rows, which in ((mine, place[0]), (other, 1 - place[0])):
        at = pl.ds(pl.multiple_of(which * HALF, HALF), HALF)
        raw = dot_nn(rows[...], wk[...])
        raw_out[at, :] = raw
        kv_out[at, :HEAD] = norm_rope(raw, gain[...], cos[at, :], sin[at, :]).astype(bf16)
        kv_out[at, HEAD:] = dot_nn(rows[...], wv[...]).astype(bf16)


def q_kernel(place, mine, other, wq, gain, cos, sin, q_out, raw_out):
    for rows, which in ((mine, place[0]), (other, 1 - place[0])):
        at = pl.ds(pl.multiple_of(which * HALF, HALF), HALF)
        raw = dot_nn(rows[...], wq[...])
        raw_out[at, :] = raw
        for h in range(Q_HEADS):
            cols = slice(h * HEAD, (h + 1) * HEAD)
            q_out[at, cols] = norm_rope(raw[:, cols], gain[...], cos[at, :], sin[at, :]).astype(bf16)


def grad_kernel(rows, wo, out):
    got = dot_nt(rows[...], wo[...]).astype(bf16)
    for zl in range(4):
        for c in range(2):
            out[c * HALF + zl * PIECE : c * HALF + (zl + 1) * PIECE, :] = got[
                (zl * 2 + c) * PIECE : (zl * 2 + c + 1) * PIECE, :
            ]


def masks(place, key_axis):
    shape = (ROWS, ROWS)
    ahead = natural(lax.broadcasted_iota(i32, shape, key_axis)) - natural(
        lax.broadcasted_iota(i32, shape, 1 - key_axis)
    )
    everything, nothing = -4 * ROWS, 4 * ROWS
    allowed = []
    for k in range(CHUNKS):
        beyond = jnp.where(place[2] > 0, everything, nothing)
        limit = jnp.where(
            k < place[1], everything, jnp.where((k == place[1]) & (place[2] > 0), 0, beyond)
        )
        allowed.append(ahead > limit)
    allowed.append(ahead <= 0)
    return allowed


def kv_chunk(halo, own, k):
    return halo[k] if k < CHUNKS else own[...]


def out_kernel(attended, wo, out):
    got = dot_nn(attended[...], wo[...]).astype(bf16)
    for zl in range(4):
        for c in range(2):
            out[(zl * 2 + c) * PIECE : (zl * 2 + c + 1) * PIECE, :] = got[
                c * HALF + zl * PIECE : c * HALF + (zl + 1) * PIECE, :
            ]


def attention_kernel(
    place, q, halo, own, grad_rows, wo, q_raw, gain, cos, sin,
    out_part, q_back, halo_back, own_back, probs, dkv, grad, attended_out,
):
    grad_kernel(grad_rows, wo, grad)
    allowed = masks(place, 0)
    for h in range(Q_HEADS):
        cols = slice(h * HEAD, (h + 1) * HEAD)
        query, out_grad = q[:, cols], grad[:, cols]
        total = jnp.zeros((1, ROWS), f32)
        for k in range(CHUNKS + 1):
            keys = kv_chunk(halo, own, k)[:, :HEAD]
            raw = jnp.where(allowed[k], jnp.exp(dot_nt(keys, query) * score_scale), 0.0)
            total = total + jnp.sum(raw, axis=0, keepdims=True)
            probs[k] = raw
        inverse = 1.0 / total
        attended = jnp.zeros((HEAD, ROWS), f32)
        for k in range(CHUNKS + 1):
            soft = probs[k] * inverse
            probs[k] = soft
            low = soft.astype(bf16)
            attended = attended + dot_tn(kv_chunk(halo, own, k)[:, HEAD:], low)
            value_grad = dot_nn(low, out_grad)
            if h > 0:
                value_grad = value_grad + dkv[k, :, HEAD:]
            if h < Q_HEADS - 1:
                dkv[k, :, HEAD:] = value_grad
            elif k < CHUNKS:
                halo_back[k, :, HEAD:] = value_grad.astype(bf16)
            else:
                own_back[:, HEAD:] = value_grad
        attended_out[:, cols] = jnp.transpose(attended).astype(bf16)
        products = jnp.transpose(out_grad.astype(f32)) * attended.astype(bf16).astype(f32)
        dots = jnp.sum(products, axis=0, keepdims=True)
        query_grad = jnp.zeros((HEAD, ROWS), f32)
        for k in range(CHUNKS + 1):
            kv = kv_chunk(halo, own, k)
            prob_grad = dot_nt(kv[:, HEAD:], out_grad)
            score_grad = (probs[k] * (prob_grad - dots) * score_scale).astype(bf16)
            key_grad = dot_nn(score_grad, query)
            query_grad = query_grad + dot_tn(kv[:, :HEAD], score_grad)
            if h > 0:
                key_grad = key_grad + dkv[k, :, :HEAD]
            if h < Q_HEADS - 1:
                dkv[k, :, :HEAD] = key_grad
            elif k < CHUNKS:
                halo_back[k, :, :HEAD] = key_grad.astype(bf16)
            else:
                own_back[:, :HEAD] = key_grad
        q_back[:, cols] = norm_rope_back(
            q_raw[:, cols], gain[...], cos[...], sin[...], jnp.transpose(query_grad)
        ).astype(bf16)
    out_kernel(attended_out, wo, out_part)


def gather_kernel(place, back, own_back, own_out, above_out):
    own = own_back[...]
    above = jnp.zeros((ROWS, 2 * HEAD), f32)
    for k in range(CHUNKS):
        later = k > place[1]
        piece = back[k].astype(f32)
        own = own + jnp.where(later, piece, 0.0)
        above = above + jnp.where(later, 0.0, piece)
    own_out[...] = own
    above_out[...] = above.astype(bf16)


def base_kernel(q_back, wq, out):
    out[...] = dot_nt(q_back[...], wq[...])


def end_rows(place, which, base, own, below, k_raw, gain, cos, sin, wk, wv):
    at = pl.ds(pl.multiple_of(which * HALF, HALF), HALF)
    total = own[at, :] + below[at, :].astype(f32)
    key_back = norm_rope_back(k_raw[at, :], gain[...], cos[at, :], sin[at, :], total[:, :HEAD])
    return (
        base[at, :]
        + dot_nt(key_back.astype(bf16), wk[...])
        + dot_nt(total[:, HEAD:].astype(bf16), wv[...])
    )


def end_given_kernel(place, base, own, below, k_raw, gain, cos, sin, wk, wv, given):
    given[...] = end_rows(
        place, 1 - place[0], base, own, below, k_raw, gain, cos, sin, wk, wv
    ).astype(bf16)


def end_pair_kernel(place, base, own, below, k_raw, gain, cos, sin, wk, wv, arrived, pair):
    rows = end_rows(place, place[0], base, own, below, k_raw, gain, cos, sin, wk, wv)
    pair[...] = (rows + arrived[...].astype(f32)).astype(bf16)


def sum_kernel(first, pieces, out):
    total = first[...].astype(f32)
    for k in range(CHUNKS):
        total = total + pieces[k].astype(f32)
    out[...] = total.astype(bf16)


def call(kernel, outs, *operands, scratch=(), flops=0):
    in_specs = [
        pl.BlockSpec(memory_space=pltpu.SMEM if a.dtype == i32 else pltpu.VMEM) for a in operands
    ]
    shapes = [
        pltpu.HBM(shape, dtype) if kept else jax.ShapeDtypeStruct(shape, dtype)
        for shape, dtype, kept in ((*out, False)[:3] for out in outs)
    ]
    out_specs = [pl.BlockSpec(memory_space=pltpu.VMEM)] * len(shapes)
    grid = ()
    if BLOCKED:
        whole = lambda a: pl.BlockSpec(a.shape, lambda i: (0,) * len(a.shape))
        in_specs = [
            pl.BlockSpec(memory_space=pltpu.SMEM) if a.dtype == i32 else whole(a) for a in operands
        ]
        out_specs = [whole(a) for a in shapes]
        grid = (1,)
    size = sum(math.prod(a.shape) * a.dtype.itemsize for a in (*operands, *shapes))
    results = pl.pallas_call(
        kernel,
        out_shape=shapes,
        in_specs=in_specs,
        out_specs=out_specs,
        grid=grid,
        scratch_shapes=scratch,
        compiler_params=pltpu.CompilerParams(vmem_limit_bytes=VMEM_MIB * 2**20),
        cost_estimate=pl.CostEstimate(flops=flops, bytes_accessed=size, transcendentals=0),
        name=kernel.__name__,
    )(*operands)
    return results[0] if len(results) == 1 else results


def on_device(
    tokens, result_grad, query_weight, key_weight, value_weight, output_weight, query_gain, key_gain
):
    width = tokens.shape[1]
    core, y = lax.axis_index("c"), lax.axis_index("y")
    block_row = lax.axis_index(("zh", "x"))
    place = jnp.stack([core, y, block_row]).astype(i32)
    query_gain, key_gain = query_gain[None], key_gain[None]
    positions = (block_row * CHUNKS + y) * ROWS + natural(jnp.arange(ROWS, dtype=i32))
    cos, sin = rope_tables(positions)

    gradients_part = lax.all_gather(result_grad, TP, axis=0, tiled=True)
    copies = call(copies_kernel, [((CHUNKS, PIECE, width), bf16)], tokens)
    mine = lax.all_to_all(copies, "zl", 0, 0, tiled=True).reshape(HALF, width)
    other = swap_cores(mine)
    own_kv, key_raw = call(
        kv_kernel,
        [((ROWS, 2 * HEAD), bf16), ((ROWS, HEAD), f32, True)],
        place, mine, other, key_weight, value_weight, key_gain, cos, sin,
    )
    above_kv = shift_rows(own_kv, 1)
    queries, query_raw = call(
        q_kernel,
        [((ROWS, Q_HEADS * HEAD), bf16, True), ((ROWS, Q_HEADS * HEAD), f32, True)],
        place, mine, other, query_weight, query_gain, cos, sin,
    )
    targets = jnp.arange(CHUNKS, dtype=i32)
    outgoing = jnp.where((targets > y)[:, None, None], own_kv[None], above_kv[None])
    outgoing, queries = lax.optimization_barrier((outgoing, queries))
    halo = lax.all_to_all(outgoing, "y", 0, 0, tiled=True)
    halo, gradients_weight = lax.optimization_barrier((halo, output_weight))
    probs = pltpu.VMEM((CHUNKS + 1, ROWS, ROWS), f32)
    in_hbm = lambda a: pltpu.with_memory_space_constraint(a, pltpu.HBM)
    out_part, query_back, halo_back, own_back = call(
        attention_kernel,
        [
            ((ROWS, width), bf16, True),
            ((ROWS, Q_HEADS * HEAD), bf16, True),
            ((CHUNKS, ROWS, 2 * HEAD), bf16),
            ((ROWS, 2 * HEAD), f32, True),
        ],
        place, in_hbm(queries), halo, in_hbm(own_kv), in_hbm(gradients_part), in_hbm(gradients_weight),
        in_hbm(query_raw), query_gain, in_hbm(cos), in_hbm(sin),
        scratch=[
            probs,
            pltpu.VMEM((CHUNKS + 1, ROWS, 2 * HEAD), f32),
            pltpu.VMEM((ROWS, Q_HEADS * HEAD), bf16),
            pltpu.VMEM((ROWS, Q_HEADS * HEAD), bf16),
        ],
    )
    out_sum = lax.psum_scatter(out_part, TP, scatter_dimension=0, tiled=True)
    back = lax.all_to_all(halo_back, "y", 0, 0, tiled=True)
    own_sum, above_sum = call(
        gather_kernel,
        [((ROWS, 2 * HEAD), f32), ((ROWS, 2 * HEAD), bf16)],
        place, back, in_hbm(own_back),
    )
    below = shift_rows(above_sum, -1)
    base = call(base_kernel, [((ROWS, width), f32)], query_back, query_weight)
    last = (place, base, own_sum, below, key_raw, key_gain, cos, sin, key_weight, value_weight)
    given = swap_cores(call(end_given_kernel, [((HALF, width), bf16)], *last))
    pair = call(end_pair_kernel, [((HALF, width), bf16)], *last, given)
    pieces = lax.all_to_all(pair.reshape(CHUNKS, PIECE, width), "zl", 0, 0, tiled=True)
    layer_output = (tokens.astype(f32) + out_sum.astype(f32)).astype(bf16)
    tokens_grad = call(sum_kernel, [((PIECE, width), bf16)], result_grad, pieces)
    return (layer_output, tokens_grad)


def solution(mesh):
    fine = Mesh(mesh.devices.reshape(4, 4, 4, 4, 2), ALL)
    in_specs = (
        P(ALL, None),
        P(ALL, None),
        P(None, TP),
        P(None, TP),
        P(None, TP),
        P(TP, None),
        P(),
        P(),
    )
    out_specs = (P(ALL, None), P(ALL, None))
    return jax.shard_map(
        on_device, mesh=fine, in_specs=in_specs, out_specs=out_specs, check_vma=False
    )
```

```python
import math

import jax
import jax.numpy as jnp
from jax import lax
from jax.experimental import pallas as pl
from jax.experimental.pallas import tpu as pltpu
from jax.sharding import Mesh, PartitionSpec as P

WINDOW = 1024
ALL = ("zh", "x", "y", "zl", "c")
TP = ("zl", "c")

norm_epsilon = 1e-06
score_scale = 168.0 ** (-0.5)
rope_theta = 10000.0
f32 = jnp.float32
bf16 = jnp.bfloat16
i32 = jnp.int32

ROWS = 256
HALF = 128
PIECE = 32
HEAD = 128
Q_HEADS = 2
CHUNKS = 4
BLOCKED = True
VMEM_MIB = 20


def swap_cores(block):
    return lax.ppermute(block, "c", [(0, 1), (1, 0)])


def shift_rows(block, step):
    count = lax.axis_size(("zh", "x"))
    route = [(i, i + step) for i in range(count) if 0 <= i + step < count]
    return lax.ppermute(block, ("zh", "x"), route)


def natural(index):
    return ((index >> 5) & 3) * 64 + (index >> 7) * 32 + (index & 31)


def rope_tables(positions):
    half_size = HEAD // 2
    exponent = jnp.arange(half_size, dtype=f32) * (2.0 / HEAD)
    frequency = jnp.power(f32(rope_theta), -exponent)
    angles = positions.astype(f32)[:, None] * frequency[None, :]
    cosines, sines = jnp.cos(angles), jnp.sin(angles)
    return (
        jnp.concatenate([cosines, cosines], axis=1),
        jnp.concatenate([-sines, sines], axis=1),
    )


def dot_nn(a, b):
    return lax.dot_general(a, b, (((1,), (0,)), ((), ())), preferred_element_type=f32)


def dot_nt(a, b):
    return lax.dot_general(a, b, (((1,), (1,)), ((), ())), preferred_element_type=f32)


def dot_tn(a, b):
    return lax.dot_general(a, b, (((0,), (0,)), ((), ())), preferred_element_type=f32)


def norm_rope(raw, gain, cosines, sines):
    inverse = lax.rsqrt(jnp.mean(raw * raw, axis=-1, keepdims=True) + norm_epsilon)
    normed = raw * inverse * gain
    return normed * cosines + pltpu.roll(normed, HEAD // 2, 1) * sines


def norm_rope_back(raw, gain, cosines, sines, grad):
    inverse = lax.rsqrt(jnp.mean(raw * raw, axis=-1, keepdims=True) + norm_epsilon)
    normed_grad = (grad * cosines - pltpu.roll(grad, HEAD // 2, 1) * sines) * gain
    along = jnp.mean(raw * normed_grad, axis=-1, keepdims=True)
    return inverse * normed_grad - raw * (inverse * inverse * inverse * along)


def copies_kernel(tokens_ref, out_ref):
    for k in range(CHUNKS):
        out_ref[k] = tokens_ref[...]


def kv_kernel(place, mine, other, wk, wv, gain, cos, sin, kv_out, raw_out):
    for rows, which in ((mine, place[0]), (other, 1 - place[0])):
        at = pl.ds(pl.multiple_of(which * HALF, HALF), HALF)
        raw = dot_nn(rows[...], wk[...])
        raw_out[at, :] = raw
        kv_out[at, :HEAD] = norm_rope(raw, gain[...], cos[at, :], sin[at, :]).astype(bf16)
        kv_out[at, HEAD:] = dot_nn(rows[...], wv[...]).astype(bf16)


def q_kernel(place, mine, other, wq, gain, cos, sin, q_out, raw_out):
    for rows, which in ((mine, place[0]), (other, 1 - place[0])):
        at = pl.ds(pl.multiple_of(which * HALF, HALF), HALF)
        raw = dot_nn(rows[...], wq[...])
        raw_out[at, :] = raw
        for h in range(Q_HEADS):
            cols = slice(h * HEAD, (h + 1) * HEAD)
            q_out[at, cols] = norm_rope(raw[:, cols], gain[...], cos[at, :], sin[at, :]).astype(bf16)


def grad_kernel(rows, wo, out):
    got = dot_nt(rows[...], wo[...]).astype(bf16)
    for zl in range(4):
        for c in range(2):
            out[c * HALF + zl * PIECE : c * HALF + (zl + 1) * PIECE, :] = got[
                (zl * 2 + c) * PIECE : (zl * 2 + c + 1) * PIECE, :
            ]


def masks(place, key_axis):
    shape = (ROWS, ROWS)
    ahead = natural(lax.broadcasted_iota(i32, shape, key_axis)) - natural(
        lax.broadcasted_iota(i32, shape, 1 - key_axis)
    )
    everything, nothing = -4 * ROWS, 4 * ROWS
    allowed = []
    for k in range(CHUNKS):
        beyond = jnp.where(place[2] > 0, everything, nothing)
        limit = jnp.where(
            k < place[1], everything, jnp.where((k == place[1]) & (place[2] > 0), 0, beyond)
        )
        allowed.append(ahead > limit)
    allowed.append(ahead <= 0)
    return allowed


def kv_chunk(halo, own, k):
    return halo[k] if k < CHUNKS else own[...]


def out_kernel(attended, wo, out):
    got = dot_nn(attended[...], wo[...]).astype(bf16)
    for zl in range(4):
        for c in range(2):
            out[(zl * 2 + c) * PIECE : (zl * 2 + c + 1) * PIECE, :] = got[
                c * HALF + zl * PIECE : c * HALF + (zl + 1) * PIECE, :
            ]


def attention_kernel(
    place, q, halo, own, grad_rows, wo, q_raw, gain, cos, sin,
    out_part, q_back, halo_back, own_back, probs, dkv, grad, attended_out,
):
    grad_kernel(grad_rows, wo, grad)
    allowed = masks(place, 0)
    for h in range(Q_HEADS):
        cols = slice(h * HEAD, (h + 1) * HEAD)
        query, out_grad = q[:, cols], grad[:, cols]
        total = jnp.zeros((1, ROWS), f32)
        for k in range(CHUNKS + 1):
            keys = kv_chunk(halo, own, k)[:, :HEAD]
            raw = jnp.where(allowed[k], jnp.exp(dot_nt(keys, query) * score_scale), 0.0)
            total = total + jnp.sum(raw, axis=0, keepdims=True)
            probs[k] = raw
        inverse = 1.0 / total
        attended = jnp.zeros((HEAD, ROWS), f32)
        for k in range(CHUNKS + 1):
            soft = probs[k] * inverse
            probs[k] = soft
            low = soft.astype(bf16)
            attended = attended + dot_tn(kv_chunk(halo, own, k)[:, HEAD:], low)
            value_grad = dot_nn(low, out_grad)
            if h > 0:
                value_grad = value_grad + dkv[k, :, HEAD:]
            if h < Q_HEADS - 1:
                dkv[k, :, HEAD:] = value_grad
            elif k < CHUNKS:
                halo_back[k, :, HEAD:] = value_grad.astype(bf16)
            else:
                own_back[:, HEAD:] = value_grad
        attended_out[:, cols] = jnp.transpose(attended).astype(bf16)
        products = jnp.transpose(out_grad.astype(f32)) * attended.astype(bf16).astype(f32)
        dots = jnp.sum(products, axis=0, keepdims=True)
        query_grad = jnp.zeros((HEAD, ROWS), f32)
        for k in range(CHUNKS + 1):
            kv = kv_chunk(halo, own, k)
            prob_grad = dot_nt(kv[:, HEAD:], out_grad)
            score_grad = (probs[k] * (prob_grad - dots) * score_scale).astype(bf16)
            key_grad = dot_nn(score_grad, query)
            query_grad = query_grad + dot_tn(kv[:, :HEAD], score_grad)
            if h > 0:
                key_grad = key_grad + dkv[k, :, :HEAD]
            if h < Q_HEADS - 1:
                dkv[k, :, :HEAD] = key_grad
            elif k < CHUNKS:
                halo_back[k, :, :HEAD] = key_grad.astype(bf16)
            else:
                own_back[:, :HEAD] = key_grad
        q_back[:, cols] = norm_rope_back(
            q_raw[:, cols], gain[...], cos[...], sin[...], jnp.transpose(query_grad)
        ).astype(bf16)
    out_kernel(attended_out, wo, out_part)


def gather_kernel(place, back, own_back, own_out, above_out):
    own = own_back[...]
    above = jnp.zeros((ROWS, 2 * HEAD), f32)
    for k in range(CHUNKS):
        later = k > place[1]
        piece = back[k].astype(f32)
        own = own + jnp.where(later, piece, 0.0)
        above = above + jnp.where(later, 0.0, piece)
    own_out[...] = own
    above_out[...] = above.astype(bf16)


def base_kernel(q_back, wq, out):
    out[...] = dot_nt(q_back[...], wq[...])


def end_rows(place, which, base, own, below, k_raw, gain, cos, sin, wk, wv):
    at = pl.ds(pl.multiple_of(which * HALF, HALF), HALF)
    total = own[at, :] + below[at, :].astype(f32)
    key_back = norm_rope_back(k_raw[at, :], gain[...], cos[at, :], sin[at, :], total[:, :HEAD])
    return (
        base[at, :]
        + dot_nt(key_back.astype(bf16), wk[...])
        + dot_nt(total[:, HEAD:].astype(bf16), wv[...])
    )


def end_given_kernel(place, base, own, below, k_raw, gain, cos, sin, wk, wv, given):
    given[...] = end_rows(
        place, 1 - place[0], base, own, below, k_raw, gain, cos, sin, wk, wv
    ).astype(bf16)


def end_pair_kernel(place, base, own, below, k_raw, gain, cos, sin, wk, wv, arrived, pair):
    rows = end_rows(place, place[0], base, own, below, k_raw, gain, cos, sin, wk, wv)
    pair[...] = (rows + arrived[...].astype(f32)).astype(bf16)


def sum_kernel(first, pieces, out):
    total = first[...].astype(f32)
    for k in range(CHUNKS):
        total = total + pieces[k].astype(f32)
    out[...] = total.astype(bf16)


def call(kernel, outs, *operands, scratch=(), flops=0):
    in_specs = [
        pl.BlockSpec(memory_space=pltpu.SMEM if a.dtype == i32 else pltpu.VMEM) for a in operands
    ]
    shapes = [
        pltpu.HBM(shape, dtype) if kept else jax.ShapeDtypeStruct(shape, dtype)
        for shape, dtype, kept in ((*out, False)[:3] for out in outs)
    ]
    out_specs = [pl.BlockSpec(memory_space=pltpu.VMEM)] * len(shapes)
    grid = ()
    if BLOCKED:
        whole = lambda a: pl.BlockSpec(a.shape, lambda i: (0,) * len(a.shape))
        in_specs = [
            pl.BlockSpec(memory_space=pltpu.SMEM) if a.dtype == i32 else whole(a) for a in operands
        ]
        out_specs = [whole(a) for a in shapes]
        grid = (1,)
    size = sum(math.prod(a.shape) * a.dtype.itemsize for a in (*operands, *shapes))
    results = pl.pallas_call(
        kernel,
        out_shape=shapes,
        in_specs=in_specs,
        out_specs=out_specs,
        grid=grid,
        scratch_shapes=scratch,
        compiler_params=pltpu.CompilerParams(vmem_limit_bytes=VMEM_MIB * 2**20),
        cost_estimate=pl.CostEstimate(flops=flops, bytes_accessed=size, transcendentals=0),
        name=kernel.__name__,
    )(*operands)
    return results[0] if len(results) == 1 else results


def on_device(
    tokens, result_grad, query_weight, key_weight, value_weight, output_weight, query_gain, key_gain
):
    width = tokens.shape[1]
    core, y = lax.axis_index("c"), lax.axis_index("y")
    block_row = lax.axis_index(("zh", "x"))
    place = jnp.stack([core, y, block_row]).astype(i32)
    query_gain, key_gain = query_gain[None], key_gain[None]
    positions = (block_row * CHUNKS + y) * ROWS + natural(jnp.arange(ROWS, dtype=i32))
    cos, sin = rope_tables(positions)

    gradients_part = lax.all_gather(result_grad, TP, axis=0, tiled=True)
    in_hbm = lambda a: pltpu.with_memory_space_constraint(a, pltpu.HBM)
    copies = call(copies_kernel, [((CHUNKS, PIECE, width), bf16, True)], in_hbm(tokens))
    mine = lax.all_to_all(copies, "zl", 0, 0, tiled=True).reshape(HALF, width)
    other = swap_cores(mine)
    own_kv, key_raw = call(
        kv_kernel,
        [((ROWS, 2 * HEAD), bf16), ((ROWS, HEAD), f32, True)],
        place, mine, other, key_weight, value_weight, key_gain, cos, sin,
    )
    above_kv = shift_rows(own_kv, 1)
    queries, query_raw = call(
        q_kernel,
        [((ROWS, Q_HEADS * HEAD), bf16, True), ((ROWS, Q_HEADS * HEAD), f32, True)],
        place, mine, other, query_weight, query_gain, cos, sin,
    )
    targets = jnp.arange(CHUNKS, dtype=i32)
    outgoing = jnp.where((targets > y)[:, None, None], own_kv[None], above_kv[None])
    outgoing, queries = lax.optimization_barrier((outgoing, queries))
    halo = lax.all_to_all(outgoing, "y", 0, 0, tiled=True)
    halo, gradients_weight = lax.optimization_barrier((halo, output_weight))
    probs = pltpu.VMEM((CHUNKS + 1, ROWS, ROWS), f32)
    out_part, query_back, halo_back, own_back = call(
        attention_kernel,
        [
            ((ROWS, width), bf16, True),
            ((ROWS, Q_HEADS * HEAD), bf16, True),
            ((CHUNKS, ROWS, 2 * HEAD), bf16),
            ((ROWS, 2 * HEAD), f32, True),
        ],
        place, in_hbm(queries), halo, in_hbm(own_kv), in_hbm(gradients_part), in_hbm(gradients_weight),
        in_hbm(query_raw), query_gain, in_hbm(cos), in_hbm(sin),
        scratch=[
            probs,
            pltpu.VMEM((CHUNKS + 1, ROWS, 2 * HEAD), f32),
            pltpu.VMEM((ROWS, Q_HEADS * HEAD), bf16),
            pltpu.VMEM((ROWS, Q_HEADS * HEAD), bf16),
        ],
    )
    out_sum = lax.psum_scatter(out_part, TP, scatter_dimension=0, tiled=True)
    back = lax.all_to_all(halo_back, "y", 0, 0, tiled=True)
    own_sum, above_sum = call(
        gather_kernel,
        [((ROWS, 2 * HEAD), f32), ((ROWS, 2 * HEAD), bf16)],
        place, back, in_hbm(own_back),
    )
    below = shift_rows(above_sum, -1)
    base = call(base_kernel, [((ROWS, width), f32)], query_back, query_weight)
    last = (place, base, own_sum, below, key_raw, key_gain, cos, sin, key_weight, value_weight)
    given = swap_cores(call(end_given_kernel, [((HALF, width), bf16)], *last))
    pair = call(end_pair_kernel, [((HALF, width), bf16)], *last, given)
    pieces = lax.all_to_all(pair.reshape(CHUNKS, PIECE, width), "zl", 0, 0, tiled=True)
    layer_output = (tokens.astype(f32) + out_sum.astype(f32)).astype(bf16)
    tokens_grad = call(sum_kernel, [((PIECE, width), bf16)], result_grad, pieces)
    return (layer_output, tokens_grad)


def solution(mesh):
    fine = Mesh(mesh.devices.reshape(4, 4, 4, 4, 2), ALL)
    in_specs = (
        P(ALL, None),
        P(ALL, None),
        P(None, TP),
        P(None, TP),
        P(None, TP),
        P(TP, None),
        P(),
        P(),
    )
    out_specs = (P(ALL, None), P(ALL, None))
    return jax.shard_map(
        on_device, mesh=fine, in_specs=in_specs, out_specs=out_specs, check_vma=False
    )
```
